32 devices in a mesh: ctx: 8 (over y, x, core), exp: 4 (over z).
Axes of the slice: x: 2, y: 2, z: 4, core: 2. Of those that a mesh axis runs over, the one named last changes fastest.
Arguments:
- ssm_input: bfloat16 [1024, 4096], P('ctx', 'exp'), may hold values from -6 to 6
- gate_input: bfloat16 [1024, 4096], P('ctx', 'exp'), may hold values from -6 to 6
- key_proj: bfloat16 [1024, 128], P('ctx'), may hold values from -4 to 4
- query_proj: bfloat16 [1024, 128], P('ctx'), may hold values from -4 to 4
- step_size: float32 [1024, 64], P('ctx', 'exp'), may hold values from 0 to 1, as said below
- decay_rate: float32 [64], P('exp'), may hold values from 0.5 to 1.5
- head_gain: float32 [4096], P('exp'), may hold values from 0.5 to 1.5
- residual: bfloat16 [1024, 4096], P('ctx', 'exp'), may hold values from -33 to 33
- ffn_gain: float32 [4096], replicated, may hold values from 0.5 to 1.5
- gate_weight: bfloat16 [4, 4096, 12288], P('exp', None, 'ctx'), may hold values from -0.09375 to 0.09375
- up_weight: bfloat16 [4, 4096, 12288], P('exp', None, 'ctx'), may hold values from -0.09375 to 0.09375
- down_weight: bfloat16 [4, 12288, 4096], P('exp', 'ctx'), may hold values from -0.0546875 to 0.0546875
- expert_ids: int32 [1024, 2], P('ctx'), may hold values from 0 to 3, all different within a row; in each aligned block of 128 rows (0 to 127, 128 to 255, ...) at most 96 rows name the same one
- route_weight: float32 [1024, 2], P('ctx'), may hold values from 0.5 to 2
Outputs:
- block_out: bfloat16 [1024, 4096], P('ctx', 'exp')
- expert_out: bfloat16 [1024, 4096], P('ctx', 'exp')
The draws below stay inside these ranges and needn't reach their ends.
Inputs may be any that keep to these rules, and one draw needn't show every extreme that they name: `step_size`: step sizes are positive. `expert_ids`: the two experts of a token differ. In each aligned block of 128 rows (the tokens of one shard) no expert is named by more than 96 rows, and in some block one expert is named by exactly 96 rows.
All inputs are finite; a program needn't handle non-finite values.
Results may differ from the reference program's by a relative error of at most 0.022.
Values may be sent and summed in bfloat16 or wider, within the bound.
A program may use at most 128 MiB of HBM per device.

```python
import math
import jax
import jax.numpy as jnp
import numpy as np
from jax import lax

D = 4096
HEADS = 64
NSTATE = 128
FF = 12288
L_DEV = 128
CONTEXT_LENGTH = 1024
EXPERTS = 4
CAP = 96


def draw_step_size(key, part):
    gradual_prng_seed, coarse_prng_seed, cluster_prng_seed = jax.random.split(key, 3)
    slow_share = 0.5
    slow_heads = jax.random.uniform(gradual_prng_seed, (HEADS,)) < slow_share
    background_intensity = jnp.where(slow_heads, 0.3 / CONTEXT_LENGTH, 1.0 / 40.0)
    perturbation_magnitude = jnp.exp(jax.random.uniform(coarse_prng_seed, (CONTEXT_LENGTH, HEADS), minval=-0.69, maxval=0.69))
    cluster_location = jax.random.randint(cluster_prng_seed, (2,), 0, CONTEXT_LENGTH)
    element_location = jnp.arange(CONTEXT_LENGTH)
    cluster_occurrences = jnp.any(element_location[:, None] == cluster_location[None, :], axis=1).astype(jnp.float32) * 0.45
    return (background_intensity[None, :] * perturbation_magnitude + cluster_occurrences[:, None]).astype(jnp.float32)


def draw_residual(key, part):
    key_column, key_row, key_entry = jax.random.split(key, 3)
    column_ramp = 1.0 + 2.0 * jnp.arange(D, dtype=jnp.float32) / D
    column_scale = column_ramp * jnp.exp(jax.random.uniform(key_column, (D,), minval=0.0, maxval=math.log(4.0)))
    row_scale = jnp.exp(jax.random.uniform(key_row, (CONTEXT_LENGTH, 1), minval=0.0, maxval=math.log(3.0)))
    entries = jax.random.truncated_normal(key_entry, -6.0, 6.0, (CONTEXT_LENGTH, D))
    return (0.15 * entries * row_scale * column_scale[None, :]).astype(jnp.bfloat16)


def shard_levels(own_key, dims, cuts, low, largest):
    def one(position, shards_of):
        heights = jax.random.uniform(jax.random.fold_in(jax.random.fold_in(own_key, 6), position), (shards_of,), jnp.float32, low / len(cuts), largest / len(cuts))
        return jnp.repeat(jnp.exp(heights), dims[position] // shards_of).reshape((-1,) + (1,) * (len(dims) - position - 1))

    factor_of = one(*cuts[0])
    for cut in cuts[1:]:
        factor_of = factor_of * one(*cut)
    return factor_of


def assign_block(rng, own, number, rows, count, top, limit, lean):
    sequence = jax.random.permutation(rng, count)
    packed, usual = portions_of(count, rows * top, limit, lean, True), portions_of(count, rows * top, limit, lean, False)
    places = jnp.arange(count)

    def named(lengths, turn):
        used = int((lengths > 0).sum())
        fixed = max(1, used // 4)
        moved = fixed + (places - fixed + turn * (used - fixed)) % max(1, count - fixed)
        return jnp.zeros((count,), jnp.int32).at[sequence[jnp.where(places < fixed, places, moved)]].set(jnp.asarray(lengths, jnp.int32))

    lengths = jnp.where(number % 4 == 0, named(packed, number // 4), named(usual, number - number // 4 - 1))
    mixed = jax.random.permutation(jax.random.fold_in(own, 3), count)
    giver, sink = mixed[0:count // 2 * 2:2], mixed[1:count // 2 * 2:2]
    margin = jnp.minimum(lengths[giver] - 1, limit - lengths[sink]) // 2
    margin = jnp.where((giver == sequence[0]) | (sink == sequence[0]) | (lengths[sink] == 0), 0, jnp.maximum(margin, 0))
    moved = jax.random.randint(jax.random.fold_in(own, 4), (count // 2,), 0, 1 << 20) % (margin + 1)
    lengths = lengths.at[giver].add(-moved).at[sink].add(moved)
    items = jnp.searchsorted(jnp.cumsum(lengths), jnp.arange(rows * top), side="right").astype(jnp.int32)
    table = items.reshape(top, rows).T
    table = table[jax.random.permutation(jax.random.fold_in(own, 1), rows)]
    turn = jax.random.randint(jax.random.fold_in(own, 2), (rows, 1), 0, top)
    return jnp.take_along_axis(table, (jnp.arange(top)[None, :] + turn) % top, axis=1)


def portions_of(amount, total, bound, skew, full):
    loads = [(1 << 20) // math.isqrt(grade ** skew) + 1 for grade in range(1, amount + 1)]
    largest = bound if full else min(bound, max(-(-total // amount), total * loads[0] // sum(loads)))
    least = 1 if total - largest >= amount - 1 else 0
    counts, rest = [largest] + [least] * (amount - 1), total - largest - least * (amount - 1)
    while rest > 0:
        candidates = [i for i in range(1, amount) if counts[i] < largest] or [i for i in range(1, amount) if counts[i] < bound]
        mass, remaining = sum([loads[i] for i in candidates]), rest
        for i in candidates:
            addition = min(bound - counts[i], max(1, remaining * loads[i] // mass), rest)
            counts[i] = counts[i] + addition
            rest = rest - addition
    return np.array(counts)


def scatter_about(rng, dims, width, limit, shards=(), kind=jnp.bfloat16):
    gain = shard_levels(rng, dims, shards, -0.22, 0.18) if shards else 1.0
    drawn = jax.random.normal(rng, dims, jnp.float32) * width * gain
    return jnp.minimum(jnp.maximum(drawn, -limit), limit).astype(kind)


def setup_inputs(seed: int = 0) -> dict:
    arg_keys = jax.random.split(jax.random.key(seed), 15)
    ssm_input = scatter_about(arg_keys[0], (CONTEXT_LENGTH, D), 1.0, 6.0, ((0, 8), (1, 4)))
    gate_input = scatter_about(arg_keys[1], (CONTEXT_LENGTH, D), 1.0, 6.0, ((0, 8), (1, 4)))
    key_proj = scatter_about(arg_keys[2], (CONTEXT_LENGTH, NSTATE), 0.3, 4.0, ((0, 8),))
    query_proj = scatter_about(arg_keys[3], (CONTEXT_LENGTH, NSTATE), 0.3, 4.0, ((0, 8),))
    step_size = draw_step_size(jax.random.fold_in(arg_keys[14], 71), 0)
    decay_rate = jnp.clip(jnp.exp(math.log(1.5) - 1.0986123 * jax.random.uniform(arg_keys[5], (HEADS,), jnp.float32) ** shard_levels(arg_keys[5], (HEADS,), ((0, 4),), -0.2, 0.2)), 0.5, 1.5)
    head_gain = jnp.clip(1.0 + 0.1 * jax.random.normal(arg_keys[6], (D,), jnp.float32), 0.5, 1.5)
    residual = draw_residual(jax.random.fold_in(arg_keys[14], 71), 0)
    ffn_gain = jnp.clip(1.0 + 0.1 * jax.random.normal(arg_keys[8], (D,), jnp.float32), 0.5, 1.5)
    gate_weight = scatter_about(arg_keys[9], (EXPERTS, D, FF), D ** -0.5, 0.09375, ((0, 4), (2, 8)))
    up_weight = scatter_about(arg_keys[10], (EXPERTS, D, FF), D ** -0.5, 0.09375, ((0, 4), (2, 8)))
    down_weight = scatter_about(arg_keys[11], (EXPERTS, FF, D), FF ** -0.5, 0.0546875, ((0, 4), (1, 8)))
    expert_ids_keys = jax.random.split(jax.random.fold_in(arg_keys[12], 1), CONTEXT_LENGTH // L_DEV)
    expert_ids_turns = jax.random.permutation(jax.random.fold_in(arg_keys[12], 3), CONTEXT_LENGTH // L_DEV)
    expert_ids = jax.vmap(lambda own, number: assign_block(jax.random.fold_in(arg_keys[12], 2), own, number, L_DEV, EXPERTS, 2, CAP, 2))(expert_ids_keys, expert_ids_turns).reshape((CONTEXT_LENGTH, 2))
    route_weight = jnp.clip(jnp.exp(math.log(2.0) - 1.3862944 * jax.random.uniform(arg_keys[13], (CONTEXT_LENGTH, 2), jnp.float32) ** shard_levels(arg_keys[13], (CONTEXT_LENGTH, 2), ((0, 8),), -0.2, 0.2)), 0.5, 2.0)
    return {"ssm_input": ssm_input, "gate_input": gate_input, "key_proj": key_proj, "query_proj": query_proj, "step_size": step_size, "decay_rate": decay_rate, "head_gain": head_gain, "residual": residual, "ffn_gain": ffn_gain, "gate_weight": gate_weight, "up_weight": up_weight, "down_weight": down_weight, "expert_ids": expert_ids, "route_weight": route_weight}


precise = lax.Precision.HIGHEST

def local_block(ssm_piece, key_piece, query_piece, step_piece, decay_rate, head_count):
    row_count = ssm_piece.shape[0]
    head_width = ssm_piece.shape[1] // head_count
    values = ssm_piece.astype(jnp.float32).reshape(row_count, head_count, head_width)
    key_vals = key_piece.astype(jnp.float32)
    queries = query_piece.astype(jnp.float32)
    log_steps = -step_piece * decay_rate[None, :]
    running = jnp.cumsum(log_steps, axis=0)
    scores = jnp.dot(queries, key_vals.T, precision=precise)
    causal = (jnp.arange(row_count)[:, None] >= jnp.arange(row_count)[None, :])[:, :, None]
    spacing = running[:, None, :] - running[None, :, :]
    decays = jnp.where(causal, jnp.exp(jnp.where(causal, spacing, 0.0)), 0.0)
    within = jnp.einsum('tsh,ts,shp->thp', decays, scores, values, precision=precise)
    overall = running[-1]
    fading = jnp.exp(overall[None, :] - running)
    states = jnp.einsum('sh,shp,sn->hpn', fading, values, key_vals, precision=precise)
    return (within, running, overall, states)

def route_tables(expert_ids, route_weight, experts, capacity):
    matched = expert_ids[None, :, :] == experts[:, None, None]
    member = jnp.any(matched, axis=2).astype(jnp.int32)
    gate_sum = lax.optimization_barrier(jnp.sum(jnp.where(matched, route_weight[None, :, :], 0.0), axis=2))
    slot_index = jnp.cumsum(member, axis=1) - 1
    positions = jnp.arange(capacity, dtype=jnp.int32)
    routing = ((slot_index[:, None, :] == positions[None, :, None]) & (member[:, None, :] > 0)).astype(jnp.float32)
    slot_weight = jnp.einsum('nkt,nt->nk', routing, gate_sum, precision=precise)
    return (routing, slot_weight)

def reference(ssm_input, gate_input, key_proj, query_proj, step_size, decay_rate, head_gain, residual, ffn_gain, gate_weight, up_weight, down_weight, expert_ids, route_weight):
    blocks = CONTEXT_LENGTH // L_DEV
    head_width = D // HEADS

    def state_step(incoming, block_in):
        within, running, overall, states = local_block(block_in[0], block_in[1], block_in[2], block_in[3], decay_rate, HEADS)
        carried = jnp.einsum('th,hpn,tn->thp', jnp.exp(running), incoming, block_in[2].astype(jnp.float32), precision=precise)
        following = jnp.exp(overall)[:, None, None] * incoming + states
        return (following, within + carried)
    initial = jnp.zeros((HEADS, head_width, NSTATE), jnp.float32)
    pieces = (ssm_input.reshape(blocks, L_DEV, D), key_proj.reshape(blocks, L_DEV, NSTATE), query_proj.reshape(blocks, L_DEV, NSTATE), step_size.reshape(blocks, L_DEV, HEADS))
    ignored, outputs = lax.scan(state_step, initial, pieces)
    mixer_out = outputs.reshape(CONTEXT_LENGTH, HEADS, head_width)
    gated_out = mixer_out * jax.nn.silu(gate_input.astype(jnp.float32)).reshape(CONTEXT_LENGTH, HEADS, head_width)
    inv_rms = lax.rsqrt(lax.optimization_barrier(jnp.mean(gated_out * gated_out, axis=2, keepdims=True)) + 1e-05)
    normed = (gated_out * inv_rms).reshape(CONTEXT_LENGTH, D) * head_gain[None, :]
    block_out = (residual.astype(jnp.float32) + normed).astype(jnp.bfloat16)
    widened = block_out.astype(jnp.float32)
    ffn_input = (widened * lax.rsqrt(lax.optimization_barrier(jnp.mean(widened * widened, axis=1, keepdims=True)) + 1e-06) * ffn_gain[None, :]).astype(jnp.bfloat16)
    slice_width = FF // blocks
    shard_ids = expert_ids.reshape(blocks, L_DEV, 2)
    shard_weight = route_weight.reshape(blocks, L_DEV, 2)
    shard_in = ffn_input.astype(jnp.float32).reshape(blocks, L_DEV, D)

    def one_expert(combined, expert):

        def per_shard(shard_rows, shard_gates):
            return route_tables(shard_rows, shard_gates, jnp.reshape(expert, (1,)), CAP)
        tables, weights = jax.vmap(per_shard)(shard_ids, shard_weight)
        tables = tables[:, 0]
        weights = weights[:, 0]
        chosen = jnp.einsum('ckt,ctd->ckd', tables, shard_in, precision=precise).astype(jnp.bfloat16).reshape(blocks * CAP, D)
        gate_all = gate_weight[expert]
        up_all = up_weight[expert]
        down_all = down_weight[expert]

        def one_slice(running_sum, slice_index):
            offset = slice_index * slice_width
            gate_part = lax.dynamic_slice_in_dim(gate_all, offset, slice_width, 1)
            up_part = lax.dynamic_slice_in_dim(up_all, offset, slice_width, 1)
            down_part = lax.dynamic_slice_in_dim(down_all, offset, slice_width, 0)
            hidden = (jax.nn.silu(jnp.dot(chosen, gate_part, preferred_element_type=jnp.float32)) * jnp.dot(chosen, up_part, preferred_element_type=jnp.float32)).astype(jnp.bfloat16)
            partial_value = jnp.dot(hidden, down_part, preferred_element_type=jnp.float32).astype(jnp.bfloat16)
            return (running_sum + lax.optimization_barrier(partial_value).astype(jnp.float32), None)
        summed, unused = lax.scan(one_slice, jnp.zeros((blocks * CAP, D), jnp.float32), jnp.arange(blocks, dtype=jnp.int32))
        result = lax.optimization_barrier(summed.astype(jnp.bfloat16)).astype(jnp.float32).reshape(blocks, CAP, D)
        returned = jnp.einsum('ckt,ck,ckd->ctd', tables, weights, result, precision=precise)
        return (combined + returned.reshape(CONTEXT_LENGTH, D), None)
    combined, unused = lax.scan(one_expert, jnp.zeros((CONTEXT_LENGTH, D), jnp.float32), jnp.arange(EXPERTS, dtype=jnp.int32))
    return (block_out, combined.astype(jnp.bfloat16))
```

```python
import functools
import math

import jax
import jax.numpy as jnp
from jax import lax
from jax.experimental import pallas as pl
from jax.experimental.pallas import tpu as pltpu
from jax.sharding import PartitionSpec as P

precise = lax.Precision.HIGHEST


def carried_in(shard, axis, combine, identity):
    length, mine = (lax.axis_size(axis), lax.axis_index(axis))
    everything = jax.tree.map(
        lambda part, kind: lax.all_gather(part.astype(kind), axis),
        shard,
        (jnp.bfloat16, jnp.bfloat16),
    )
    start = jax.tree.map(
        lambda part, zero: jnp.broadcast_to(jnp.asarray(zero, part.dtype), part.shape),
        shard,
        identity,
    )

    def lap(k, before):
        reached = k < mine
        new = combine(
            before, jax.tree.map(lambda part, own: part[k].astype(own.dtype), everything, shard)
        )
        return jax.tree.map(lambda a, b: jnp.where(reached, a, b), new, before)

    return lax.fori_loop(0, length, lap, start)


def local_block(ssm_piece, key_piece, query_piece, step_piece, decay_rate, head_count):
    row_count = ssm_piece.shape[0]
    head_width = ssm_piece.shape[1] // head_count
    values = ssm_piece.astype(jnp.float32).reshape(row_count, head_count, head_width)
    key_vals = key_piece.astype(jnp.float32)
    queries = query_piece.astype(jnp.float32)
    log_steps = -step_piece * decay_rate[None, :]
    running = jnp.cumsum(log_steps, axis=0)
    scores = jnp.dot(queries, key_vals.T, precision=precise)
    causal = (jnp.arange(row_count)[:, None] >= jnp.arange(row_count)[None, :])[:, :, None]
    spacing = running[:, None, :] - running[None, :, :]
    decays = jnp.where(causal, jnp.exp(jnp.where(causal, spacing, 0.0)), 0.0)
    within = jnp.einsum("tsh,ts,shp->thp", decays, scores, values, precision=precise)
    overall = running[-1]
    fading = jnp.exp(overall[None, :] - running)
    states = jnp.einsum("sh,shp,sn->hpn", fading, values, key_vals, precision=precise)
    return (within, running, overall, states)


def route_tables(expert_ids, route_weight, experts, capacity):
    matched = expert_ids[None, :, :] == experts[:, None, None]
    member = jnp.any(matched, axis=2).astype(jnp.int32)
    gate_sum = jnp.sum(jnp.where(matched, route_weight[None, :, :], 0.0), axis=2)
    slot_index = jnp.cumsum(member, axis=1) - 1
    positions = jnp.arange(capacity, dtype=jnp.int32)
    routing = (
        (slot_index[:, None, :] == positions[None, :, None]) & (member[:, None, :] > 0)
    ).astype(jnp.float32)
    return (routing, gate_sum)


MESH = pl.DeviceIdType.MESH


def expert_kernel(
    wide,
    tall,
    picked_ref,
    gain_ref,
    gate_hbm,
    up_hbm,
    down_hbm,
    out_ref,
    arrived,
    rows_ref,
    gate_ref,
    up_ref,
    down_ref,
    hidden_ref,
    pair_ref,
    first_ref,
    second_ref,
    leaving,
    load_sem,
    in_sem,
    one_sem,
    two_sem,
    twin_sem,
    swap_sem,
    fold_sem,
    last_sem,
    out_sem,
):
    me, z = lax.axis_index("ctx"), lax.axis_index("exp")
    planes, count, width = picked_ref.shape
    half = rows_ref.shape[3]
    depth = gate_ref.shape[1]
    model = gate_ref.shape[0]
    core = lax.rem(me, 2)
    chip = me // 2
    x, y = lax.rem(chip, wide), chip // wide
    sizes = (wide, tall)

    def chip_at(i, j):
        return lax.rem(y + j + tall, tall) * wide + lax.rem(x + i + wide, wide)

    def ctx_at(i, j):
        return chip_at(i, j) * 2 + core

    def send(source, target, sem, index, where):
        return pltpu.make_async_remote_copy(
            src_ref=source,
            dst_ref=target,
            send_sem=sem.at[(0,) + index],
            recv_sem=sem.at[(1,) + index],
            device_id=where,
            device_id_type=MESH,
        )

    def along(h, first, second):
        return (first, second) if h == 0 else (second, first)

    twin = {"ctx": me + 1 - 2 * core}
    partners = [twin]
    partners += [{"ctx": ctx_at(i, 0)} for i in range(1, wide)]
    partners += [{"ctx": ctx_at(0, j)} for j in range(1, tall)]
    partners += [{"exp": lax.rem(z + d, planes)} for d in range(1, planes)]
    barrier = pltpu.get_barrier_semaphore()
    for partner in partners:
        pl.semaphore_signal(barrier, inc=1, device_id=partner, device_id_type=MESH)
    pl.semaphore_wait(barrier, len(partners))

    inward = []
    for d in range(1, planes):
        goal = lax.rem(z + d, planes)
        inward.append(send(picked_ref.at[goal], arrived.at[z], in_sem, (d,), {"exp": goal}))
        inward[-1].start()
    loads = [
        pltpu.make_async_copy(gate_hbm, gate_ref, load_sem.at[0]),
        pltpu.make_async_copy(up_hbm, up_ref, load_sem.at[1]),
        pltpu.make_async_copy(down_hbm, down_ref, load_sem.at[2]),
    ]
    for load in loads:
        load.start()
    arrived[z] = picked_ref[z]
    for copy in inward:
        copy.wait_recv()
    total = jnp.zeros((count, 1), jnp.float32)
    for s in range(planes):
        part = arrived[s].astype(jnp.float32)
        total = total + jnp.sum(part * part, axis=1, keepdims=True)
    scale = lax.rsqrt(total / model + 1e-06)
    for s in range(planes):
        h, start = (s * width) // half, (s * width) % half
        rows_ref[h, me, :, start : start + width] = (
            arrived[s].astype(jnp.float32) * scale * gain_ref[s : s + 1, :]
        ).astype(jnp.bfloat16)

    ones, twos, twins = {}, {}, {}
    for h in range(2):
        major, minor = along(h, wide, tall)
        for k in range(1, major):
            i, j = along(h, k, 0)
            block = rows_ref.at[h, me]
            ones[h, k] = send(block, block, one_sem, (h, k), {"ctx": ctx_at(i, j)})
            ones[h, k].start()

    def pass_on(h, i, j):
        block = rows_ref.at[h, ctx_at(-i, -j)]
        twins[h, i, j] = send(block, block, twin_sem, (h, i, j), twin)
        twins[h, i, j].start()

    def turn(h, k):
        major, minor = along(h, wide, tall)
        i, j = along(h, k, 0)
        block = rows_ref.at[h, ctx_at(-i, -j)]
        for m in range(1, minor):
            a, b = along(h, 0, m)
            twos[h, k, m] = send(block, block, two_sem, (h, k, m), {"ctx": ctx_at(a, b)})
            twos[h, k, m].start()

    for h in range(2):
        turn(h, 0)
    for h in range(2):
        pass_on(h, 0, 0)

    step = 256 if depth % 256 == 0 else 128

    def raise_rows(i, j):
        group = j * wide + i
        blocks = pl.ds(chip_at(-i, -j) * 2, 2)

        @pl.loop(0, depth // step)
        def _(t):
            cols = pl.ds(pl.multiple_of(t * step, step), step)

            def product(w_ref):
                value = None
                for h in range(2):
                    left = rows_ref[h, blocks].reshape(2 * count, half)
                    term = jnp.dot(
                        left,
                        w_ref[h * half : (h + 1) * half, cols],
                        preferred_element_type=jnp.float32,
                    )
                    value = term if value is None else value + term
                return value

            gate = product(gate_ref)
            hidden_ref[group, :, cols] = (gate * jax.nn.sigmoid(gate) * product(up_ref)).astype(
                jnp.bfloat16
            )

    order = sorted(
        [(i, j) for i in range(wide) for j in range(tall)], key=lambda o: (o[0] + o[1], o)
    )
    loads[0].wait()
    loads[1].wait()
    for h in range(2):
        twins[h, 0, 0].wait_recv()
    raise_rows(0, 0)
    for h in range(2):
        for k in range(1, sizes[h]):
            ones[h, k].wait_recv()
            turn(h, k)
            i, j = along(h, k, 0)
            pass_on(h, i, j)
    for h in range(2):
        for m in range(1, sizes[1 - h]):
            twos[h, 0, m].wait_recv()
            i, j = along(h, 0, m)
            pass_on(h, i, j)
    for i, j in order[1:]:
        for h in range(2):
            k, m = along(h, i, j)
            if k > 0 and m > 0:
                twos[h, k, m].wait_recv()
                pass_on(h, i, j)
        for h in range(2):
            twins[h, i, j].wait_recv()
        raise_rows(i, j)
    for copy in list(ones.values()) + list(twos.values()) + list(twins.values()):
        copy.wait_send()

    swaps, folds, lasts = {}, {}, {}
    loads[2].wait()

    def lower_rows(i, j):
        group = lax.rem(tall - j, tall) * wide + lax.rem(wide - i, wide)
        group = ((tall - j) % tall) * wide + (wide - i) % wide
        base = chip_at(i, j) * 2
        for h in range(2):

            @pl.loop(0, half // 256)
            def _(t):
                cols = pl.ds(pl.multiple_of(t * 256, 256), 256)
                source = pl.ds(pl.multiple_of(h * half + t * 256, 256), 256)
                value = jnp.dot(
                    hidden_ref[group], down_ref[:, source], preferred_element_type=jnp.float32
                )
                rows_ref[h, pl.ds(base, 2), :, cols] = value.astype(jnp.bfloat16).reshape(
                    2, count, 256
                )

            swaps[h, i, j] = send(
                rows_ref.at[h, base + 1 - core],
                pair_ref.at[h, j * wide + i],
                swap_sem,
                (h, i, j),
                twin,
            )
            swaps[h, i, j].start()

    def add_into(target, other):
        @pl.loop(0, count // 16)
        def _(t):
            some = pl.ds(pl.multiple_of(t * 16, 16), 16)
            target[some, :] = (
                target[some, :].astype(jnp.float32) + other[some, :].astype(jnp.float32)
            ).astype(jnp.bfloat16)

    def settle(i, j):
        for h in range(2):
            swaps[h, i, j].wait_recv()
            own = rows_ref.at[h, ctx_at(i, j)]
            add_into(own, pair_ref.at[h, j * wide + i])
            k, m = along(h, i, j)
            if k > 0:
                a, b = along(h, k, 0)
                folds[h, k, m] = send(
                    own, first_ref.at[h, k, m], fold_sem, (h, k, m), {"ctx": ctx_at(a, b)}
                )
                folds[h, k, m].start()

    goals = order[::-1]
    for number, goal in enumerate(goals):
        lower_rows(*goal)
        if number:
            settle(*goals[number - 1])
    settle(*goals[-1])
    for h in range(2):
        major, minor = along(h, wide, tall)
        for m in list(range(1, minor)) + [0]:
            i, j = along(h, 0, m)
            own = rows_ref.at[h, ctx_at(i, j)]
            for k in range(1, major):
                folds[h, k, m].wait_recv()
                add_into(own, first_ref.at[h, k, m])
            if m:
                lasts[h, m] = send(
                    own, second_ref.at[h, m], last_sem, (h, m), {"ctx": ctx_at(i, j)}
                )
                lasts[h, m].start()
    for h in range(2):
        for m in range(1, sizes[1 - h]):
            lasts[h, m].wait_recv()
            add_into(rows_ref.at[h, me], second_ref.at[h, m])
    for s in range(planes):
        h, start = (s * width) // half, (s * width) % half
        leaving[s] = rows_ref[h, me, :, start : start + width]
    outward = []
    for d in range(1, planes):
        goal = lax.rem(z + d, planes)
        outward.append(send(leaving.at[goal], out_ref.at[z], out_sem, (d,), {"exp": goal}))
        outward[-1].start()
    out_ref[z] = leaving[z]
    for copy in outward:
        copy.wait_recv()
    for copy in inward + outward + list(swaps.values()) + list(folds.values()):
        copy.wait_send()
    for copy in lasts.values():
        copy.wait_send()


def expert_rows(picked, gain, gate_here, up_here, down_here):
    shards, planes = lax.axis_size("ctx"), lax.axis_size("exp")
    chips = shards // 2
    wide = math.isqrt(chips)
    tall = chips // wide
    _, count, width = picked.shape
    model, depth = gate_here.shape
    half = model // 2
    most = max(wide, tall)
    vmem = pl.BlockSpec(memory_space=pltpu.VMEM)
    hbm = pl.BlockSpec(memory_space=pl.ANY)
    sems = pltpu.SemaphoreType.DMA
    return pl.pallas_call(
        functools.partial(expert_kernel, wide, tall),
        out_shape=jax.ShapeDtypeStruct((planes, count, width), jnp.bfloat16),
        in_specs=[vmem, vmem, hbm, hbm, hbm],
        out_specs=vmem,
        scratch_shapes=[
            pltpu.VMEM((planes, count, width), jnp.bfloat16),
            pltpu.VMEM((2, shards, count, half), jnp.bfloat16),
            pltpu.VMEM((model, depth), jnp.bfloat16),
            pltpu.VMEM((model, depth), jnp.bfloat16),
            pltpu.VMEM((depth, model), jnp.bfloat16),
            pltpu.VMEM((chips, 2 * count, depth), jnp.bfloat16),
            pltpu.VMEM((2, chips, count, half), jnp.bfloat16),
            pltpu.VMEM((2, most, most, count, half), jnp.bfloat16),
            pltpu.VMEM((2, most, count, half), jnp.bfloat16),
            pltpu.VMEM((planes, count, width), jnp.bfloat16),
            sems((3,)),
            sems((2, planes)),
            sems((2, 2, most)),
            sems((2, 2, most, most)),
            sems((2, 2, wide, tall)),
            sems((2, 2, wide, tall)),
            sems((2, 2, most, most)),
            sems((2, 2, most)),
            sems((2, planes)),
        ],
        compiler_params=pltpu.CompilerParams(
            collective_id=0, has_side_effects=True, vmem_limit_bytes=60 * 1024 * 1024
        ),
        cost_estimate=pl.CostEstimate(
            flops=6 * shards * count * model * depth,
            bytes_accessed=6 * model * depth,
            transcendentals=shards * count * depth,
        ),
    )(picked, gain, gate_here, up_here, down_here)


def join_states(earlier, later):
    return (earlier[0] + later[0], jnp.exp(later[0])[:, None, None] * earlier[1] + later[1])


def on_device(
    ssm_input,
    gate_input,
    key_proj,
    query_proj,
    step_size,
    decay_rate,
    head_gain,
    residual,
    ffn_gain,
    gate_weight,
    up_weight,
    down_weight,
    expert_ids,
    route_weight,
):
    head_count = step_size.shape[1]
    row_count, channels = ssm_input.shape
    head_width = channels // head_count
    within, running, overall, states = local_block(
        ssm_input, key_proj, query_proj, step_size, decay_rate, head_count
    )
    prefix = carried_in(
        (overall, states), "ctx", join_states, (jnp.zeros_like(overall), jnp.zeros_like(states))
    )
    before = prefix[1]
    carried = jnp.einsum(
        "th,hpn,tn->thp",
        jnp.exp(running),
        before,
        query_proj.astype(jnp.float32),
        precision=precise,
    )
    mixer_out = within + carried
    gated_out = mixer_out * jax.nn.silu(gate_input.astype(jnp.float32)).reshape(
        row_count, head_count, head_width
    )
    inv_rms = lax.rsqrt(jnp.mean(gated_out * gated_out, axis=2, keepdims=True) + 1e-05)
    normed = (gated_out * inv_rms).reshape(row_count, channels) * head_gain[None, :]
    block_out = (residual.astype(jnp.float32) + normed).astype(jnp.bfloat16)
    exp_count = lax.axis_size("exp")
    capacity = 3 * row_count // exp_count
    tables, gate_sum = route_tables(
        expert_ids, route_weight, jnp.arange(exp_count, dtype=jnp.int32), capacity
    )
    rows = exp_count * capacity
    picked = jnp.dot(
        tables.reshape(rows, row_count).astype(jnp.bfloat16),
        block_out,
        preferred_element_type=jnp.float32,
    ).astype(jnp.bfloat16)
    returned = expert_rows(
        picked.reshape(exp_count, capacity, channels),
        ffn_gain.reshape(exp_count, channels),
        gate_weight[0],
        up_weight[0],
        down_weight[0],
    )
    spread = jnp.einsum(
        "ekt,ekf->etf",
        tables.astype(jnp.bfloat16),
        returned,
        preferred_element_type=jnp.float32,
    )
    expert_out = jnp.sum(spread * gate_sum[:, :, None], axis=0).astype(jnp.bfloat16)
    return (block_out, expert_out)


def solution(mesh):
    placed = (
        P("ctx", "exp"),
        P("ctx", "exp"),
        P("ctx", None),
        P("ctx", None),
        P("ctx", "exp"),
        P("exp"),
        P("exp"),
        P("ctx", "exp"),
        P(),
        P("exp", None, "ctx"),
        P("exp", None, "ctx"),
        P("exp", "ctx", None),
        P("ctx", None),
        P("ctx", None),
    )
    return jax.shard_map(
        on_device,
        mesh=mesh,
        in_specs=placed,
        out_specs=(P("ctx", "exp"), P("ctx", "exp")),
        check_vma=False,
    )
```

```python
import functools
import math

import jax
import jax.numpy as jnp
from jax import lax
from jax.experimental import pallas as pl
from jax.experimental.pallas import tpu as pltpu
from jax.sharding import PartitionSpec as P

precise = lax.Precision.HIGHEST


def local_block(ssm_piece, key_piece, query_piece, step_piece, decay_rate, head_count):
    row_count = ssm_piece.shape[0]
    head_width = ssm_piece.shape[1] // head_count
    values = ssm_piece.astype(jnp.float32).reshape(row_count, head_count, head_width)
    key_vals = key_piece.astype(jnp.float32)
    queries = query_piece.astype(jnp.float32)
    log_steps = -step_piece * decay_rate[None, :]
    running = jnp.cumsum(log_steps, axis=0)
    scores = jnp.dot(queries, key_vals.T, precision=precise)
    causal = (jnp.arange(row_count)[:, None] >= jnp.arange(row_count)[None, :])[:, :, None]
    spacing = running[:, None, :] - running[None, :, :]
    decays = jnp.where(causal, jnp.exp(jnp.where(causal, spacing, 0.0)), 0.0)
    within = jnp.einsum("tsh,ts,shp->thp", decays, scores, values, precision=precise)
    overall = running[-1]
    fading = jnp.exp(overall[None, :] - running)
    states = jnp.einsum("sh,shp,sn->hpn", fading, values, key_vals, precision=precise)
    return (within, running, overall, states)


def route_tables(expert_ids, route_weight, experts, capacity):
    matched = expert_ids[None, :, :] == experts[:, None, None]
    member = jnp.any(matched, axis=2).astype(jnp.int32)
    gate_sum = jnp.sum(jnp.where(matched, route_weight[None, :, :], 0.0), axis=2)
    slot_index = jnp.cumsum(member, axis=1) - 1
    positions = jnp.arange(capacity, dtype=jnp.int32)
    routing = (
        (slot_index[:, None, :] == positions[None, :, None]) & (member[:, None, :] > 0)
    ).astype(jnp.float32)
    return (routing, gate_sum)


MESH = pl.DeviceIdType.MESH


def expert_kernel(
    wide,
    tall,
    picked_ref,
    gain_ref,
    gate_hbm,
    up_hbm,
    down_hbm,
    out_ref,
    arrived,
    rows_ref,
    gate_ref,
    up_ref,
    down_ref,
    hidden_ref,
    pair_ref,
    first_ref,
    second_ref,
    leaving,
    load_sem,
    in_sem,
    one_sem,
    two_sem,
    twin_sem,
    swap_sem,
    fold_sem,
    last_sem,
    out_sem,
):
    me, z = lax.axis_index("ctx"), lax.axis_index("exp")
    planes, count, width = picked_ref.shape
    half = rows_ref.shape[3]
    depth = gate_ref.shape[1]
    model = gate_ref.shape[0]
    core = lax.rem(me, 2)
    chip = me // 2
    x, y = lax.rem(chip, wide), chip // wide
    sizes = (wide, tall)
    pieces = 2 if count % 32 == 0 else 1
    piece = count // pieces

    def chip_at(i, j):
        return lax.rem(y + j + tall, tall) * wide + lax.rem(x + i + wide, wide)

    def ctx_at(i, j):
        return chip_at(i, j) * 2 + core

    def send(source, target, sem, index, where):
        return pltpu.make_async_remote_copy(
            src_ref=source,
            dst_ref=target,
            send_sem=sem.at[(0,) + index],
            recv_sem=sem.at[(1,) + index],
            device_id=where,
            device_id_type=MESH,
        )

    def along(h, first, second):
        return (first, second) if h == 0 else (second, first)

    twin = {"ctx": me + 1 - 2 * core}
    partners = [twin]
    partners += [{"ctx": ctx_at(i, 0)} for i in range(1, wide)]
    partners += [{"ctx": ctx_at(0, j)} for j in range(1, tall)]
    partners += [{"exp": lax.rem(z + d, planes)} for d in range(1, planes)]
    barrier = pltpu.get_barrier_semaphore()
    for partner in partners:
        pl.semaphore_signal(barrier, inc=1, device_id=partner, device_id_type=MESH)
    pl.semaphore_wait(barrier, len(partners))

    def some(r):
        return pl.ds(r * piece, piece)

    inward = {}
    for r in range(pieces):
        for d in range(1, planes):
            goal = lax.rem(z + d, planes)
            inward[d, r] = send(
                picked_ref.at[goal, some(r)],
                arrived.at[z, some(r)],
                in_sem,
                (d, r),
                {"exp": goal},
            )
            inward[d, r].start()
    loads = [
        pltpu.make_async_copy(gate_hbm, gate_ref, load_sem.at[0]),
        pltpu.make_async_copy(up_hbm, up_ref, load_sem.at[1]),
        pltpu.make_async_copy(down_hbm, down_ref, load_sem.at[2]),
    ]
    for load in loads:
        load.start()
    arrived[z] = picked_ref[z]
    ones, twos, twins = {}, {}, {}

    def pass_on(h, i, j, r):
        block = rows_ref.at[h, ctx_at(-i, -j), some(r)]
        twins[h, i, j, r] = send(block, block, twin_sem, (h, i, j, r), twin)
        twins[h, i, j, r].start()

    def turn(h, k, r):
        i, j = along(h, k, 0)
        block = rows_ref.at[h, ctx_at(-i, -j), some(r)]
        for m in range(1, sizes[1 - h]):
            a, b = along(h, 0, m)
            twos[h, k, m, r] = send(
                block, block, two_sem, (h, k, m, r), {"ctx": ctx_at(a, b)}
            )
            twos[h, k, m, r].start()

    for r in range(pieces):
        for d in range(1, planes):
            inward[d, r].wait_recv()
        total = jnp.zeros((piece, 1), jnp.float32)
        for s in range(planes):
            part = arrived[s, some(r)].astype(jnp.float32)
            total = total + jnp.sum(part * part, axis=1, keepdims=True)
        scale = lax.rsqrt(total / model + 1e-06)
        for s in range(planes):
            h, start = (s * width) // half, (s * width) % half
            rows_ref[h, me, some(r), start : start + width] = (
                arrived[s, some(r)].astype(jnp.float32) * scale * gain_ref[s : s + 1, :]
            ).astype(jnp.bfloat16)
        for h in range(2):
            for k in range(1, sizes[h]):
                i, j = along(h, k, 0)
                block = rows_ref.at[h, me, some(r)]
                ones[h, k, r] = send(
                    block, block, one_sem, (h, k, r), {"ctx": ctx_at(i, j)}
                )
                ones[h, k, r].start()
        for h in range(2):
            turn(h, 0, r)
        for h in range(2):
            pass_on(h, 0, 0, r)

    step = 256 if depth % 256 == 0 else 128

    def raise_rows(i, j):
        group = j * wide + i
        blocks = pl.ds(chip_at(-i, -j) * 2, 2)

        @pl.loop(0, depth // step)
        def _(t):
            cols = pl.ds(pl.multiple_of(t * step, step), step)

            def product(w_ref):
                value = None
                for h in range(2):
                    left = rows_ref[h, blocks].reshape(2 * count, half)
                    term = jnp.dot(
                        left,
                        w_ref[h * half : (h + 1) * half, cols],
                        preferred_element_type=jnp.float32,
                    )
                    value = term if value is None else value + term
                return value

            gate = product(gate_ref)
            hidden_ref[group, :, cols] = (gate * jax.nn.sigmoid(gate) * product(up_ref)).astype(
                jnp.bfloat16
            )

    order = sorted(
        [(i, j) for i in range(wide) for j in range(tall)], key=lambda o: (o[0] + o[1], o)
    )
    loads[0].wait()
    loads[1].wait()
    for r in range(pieces):
        for h in range(2):
            for k in range(1, sizes[h]):
                if r == 0:
                    ones[h, k, r].wait_recv()
                    turn(h, k, r)
                    pass_on(h, *along(h, k, 0), r)
    for r in range(pieces):
        for h in range(2):
            twins[h, 0, 0, r].wait_recv()
    raise_rows(0, 0)
    for r in range(1, pieces):
        for h in range(2):
            for k in range(1, sizes[h]):
                ones[h, k, r].wait_recv()
                turn(h, k, r)
                pass_on(h, *along(h, k, 0), r)
    for r in range(pieces):
        for h in range(2):
            for m in range(1, sizes[1 - h]):
                twos[h, 0, m, r].wait_recv()
                pass_on(h, *along(h, 0, m), r)
    for i, j in order[1:]:
        for r in range(pieces):
            for h in range(2):
                k, m = along(h, i, j)
                if k > 0 and m > 0:
                    twos[h, k, m, r].wait_recv()
                    pass_on(h, i, j, r)
        for r in range(pieces):
            for h in range(2):
                twins[h, i, j, r].wait_recv()
        raise_rows(i, j)
    for copy in list(ones.values()) + list(twos.values()) + list(twins.values()):
        copy.wait_send()

    swaps, folds, lasts = {}, {}, {}
    loads[2].wait()

    def lower_rows(i, j):
        group = ((tall - j) % tall) * wide + (wide - i) % wide
        base = chip_at(i, j) * 2
        for h in range(2):

            @pl.loop(0, half // 256)
            def _(t):
                cols = pl.ds(pl.multiple_of(t * 256, 256), 256)
                source = pl.ds(pl.multiple_of(h * half + t * 256, 256), 256)
                value = jnp.dot(
                    hidden_ref[group], down_ref[:, source], preferred_element_type=jnp.float32
                )
                rows_ref[h, pl.ds(base, 2), :, cols] = value.astype(jnp.bfloat16).reshape(
                    2, count, 256
                )

            swaps[h, i, j] = send(
                rows_ref.at[h, base + 1 - core],
                pair_ref.at[h, j * wide + i],
                swap_sem,
                (h, i, j),
                twin,
            )
            swaps[h, i, j].start()

    def add_into(target, other):
        @pl.loop(0, piece // 16)
        def _(t):
            few = pl.ds(pl.multiple_of(t * 16, 16), 16)
            target[few, :] = (
                target[few, :].astype(jnp.float32) + other[few, :].astype(jnp.float32)
            ).astype(jnp.bfloat16)

    def settle(i, j):
        for h in range(2):
            swaps[h, i, j].wait_recv()
        for r in range(pieces):
            for h in range(2):
                own = rows_ref.at[h, ctx_at(i, j), some(r)]
                add_into(own, pair_ref.at[h, j * wide + i, some(r)])
                k, m = along(h, i, j)
                if k > 0:
                    a, b = along(h, k, 0)
                    folds[h, k, m, r] = send(
                        own,
                        first_ref.at[h, k, m, some(r)],
                        fold_sem,
                        (h, k, m, r),
                        {"ctx": ctx_at(a, b)},
                    )
                    folds[h, k, m, r].start()

    goals = order[::-1]
    for number, goal in enumerate(goals):
        lower_rows(*goal)
        if number:
            settle(*goals[number - 1])
    settle(*goals[-1])
    for r in range(pieces):
        for h in range(2):
            major, minor = along(h, wide, tall)
            for m in range(1, minor):
                i, j = along(h, 0, m)
                own = rows_ref.at[h, ctx_at(i, j), some(r)]
                for k in range(1, major):
                    folds[h, k, m, r].wait_recv()
                    add_into(own, first_ref.at[h, k, m, some(r)])
                lasts[h, m, r] = send(
                    own,
                    second_ref.at[h, m, some(r)],
                    last_sem,
                    (h, m, r),
                    {"ctx": ctx_at(i, j)},
                )
                lasts[h, m, r].start()
    outward = {}
    for r in range(pieces):
        for h in range(2):
            own = rows_ref.at[h, me, some(r)]
            for k in range(1, sizes[h]):
                folds[h, k, 0, r].wait_recv()
                add_into(own, first_ref.at[h, k, 0, some(r)])
            for m in range(1, sizes[1 - h]):
                lasts[h, m, r].wait_recv()
                add_into(own, second_ref.at[h, m, some(r)])
        for s in range(planes):
            h, start = (s * width) // half, (s * width) % half
            leaving[s, some(r)] = rows_ref[h, me, some(r), start : start + width]
        for d in range(1, planes):
            goal = lax.rem(z + d, planes)
            outward[d, r] = send(
                leaving.at[goal, some(r)],
                out_ref.at[z, some(r)],
                out_sem,
                (d, r),
                {"exp": goal},
            )
            outward[d, r].start()
    out_ref[z] = leaving[z]
    for copy in outward.values():
        copy.wait_recv()
    for group in (inward, outward, swaps, folds, lasts):
        for copy in group.values():
            copy.wait_send()


def expert_rows(picked, gain, gate_here, up_here, down_here):
    shards, planes = lax.axis_size("ctx"), lax.axis_size("exp")
    chips = shards // 2
    wide = math.isqrt(chips)
    tall = chips // wide
    _, count, width = picked.shape
    model, depth = gate_here.shape
    half = model // 2
    most = max(wide, tall)
    vmem = pl.BlockSpec(memory_space=pltpu.VMEM)
    hbm = pl.BlockSpec(memory_space=pl.ANY)
    sems = pltpu.SemaphoreType.DMA
    return pl.pallas_call(
        functools.partial(expert_kernel, wide, tall),
        out_shape=jax.ShapeDtypeStruct((planes, count, width), jnp.bfloat16),
        in_specs=[vmem, vmem, hbm, hbm, hbm],
        out_specs=vmem,
        scratch_shapes=[
            pltpu.VMEM((planes, count, width), jnp.bfloat16),
            pltpu.VMEM((2, shards, count, half), jnp.bfloat16),
            pltpu.VMEM((model, depth), jnp.bfloat16),
            pltpu.VMEM((model, depth), jnp.bfloat16),
            pltpu.VMEM((depth, model), jnp.bfloat16),
            pltpu.VMEM((chips, 2 * count, depth), jnp.bfloat16),
            pltpu.VMEM((2, chips, count, half), jnp.bfloat16),
            pltpu.VMEM((2, most, most, count, half), jnp.bfloat16),
            pltpu.VMEM((2, most, count, half), jnp.bfloat16),
            pltpu.VMEM((planes, count, width), jnp.bfloat16),
            sems((3,)),
            sems((2, planes, 2)),
            sems((2, 2, most, 2)),
            sems((2, 2, most, most, 2)),
            sems((2, 2, wide, tall, 2)),
            sems((2, 2, wide, tall)),
            sems((2, 2, most, most, 2)),
            sems((2, 2, most, 2)),
            sems((2, planes, 2)),
        ],
        compiler_params=pltpu.CompilerParams(
            collective_id=0, has_side_effects=True, vmem_limit_bytes=60 * 1024 * 1024
        ),
        cost_estimate=pl.CostEstimate(
            flops=6 * shards * count * model * depth,
            bytes_accessed=6 * model * depth,
            transcendentals=shards * count * depth,
        ),
    )(picked, gain, gate_here, up_here, down_here)


def state_kernel(wide, tall, own_ref, all_ref, one_sem, two_sem, twin_sem):
    me = lax.axis_index("ctx")
    core = lax.rem(me, 2)
    chip = me // 2
    x, y = lax.rem(chip, wide), chip // wide
    sizes = (wide, tall)

    def ctx_at(i, j):
        return (lax.rem(y + j + tall, tall) * wide + lax.rem(x + i + wide, wide)) * 2 + core

    def send(block, sem, index, where):
        return pltpu.make_async_remote_copy(
            src_ref=block,
            dst_ref=block,
            send_sem=sem.at[(0,) + index],
            recv_sem=sem.at[(1,) + index],
            device_id=where,
            device_id_type=MESH,
        )

    def along(h, first, second):
        return (first, second) if h == 0 else (second, first)

    twin = {"ctx": me + 1 - 2 * core}
    partners = [twin]
    partners += [{"ctx": ctx_at(i, 0)} for i in range(1, wide)]
    partners += [{"ctx": ctx_at(0, j)} for j in range(1, tall)]
    barrier = pltpu.get_barrier_semaphore()
    for partner in partners:
        pl.semaphore_signal(barrier, inc=1, device_id=partner, device_id_type=MESH)
    for h in range(2):
        all_ref[h, me] = own_ref[h]
    pl.semaphore_wait(barrier, len(partners))
    ones, twos, twins = {}, {}, {}
    for h in range(2):
        for k in range(1, sizes[h]):
            i, j = along(h, k, 0)
            ones[h, k] = send(all_ref.at[h, me], one_sem, (h, k), {"ctx": ctx_at(i, j)})
            ones[h, k].start()

    def pass_on(h, i, j):
        twins[h, i, j] = send(all_ref.at[h, ctx_at(-i, -j)], twin_sem, (h, i, j), twin)
        twins[h, i, j].start()

    def turn(h, k):
        i, j = along(h, k, 0)
        block = all_ref.at[h, ctx_at(-i, -j)]
        for m in range(1, sizes[1 - h]):
            a, b = along(h, 0, m)
            twos[h, k, m] = send(block, two_sem, (h, k, m), {"ctx": ctx_at(a, b)})
            twos[h, k, m].start()

    for h in range(2):
        turn(h, 0)
    for h in range(2):
        pass_on(h, 0, 0)
    for h in range(2):
        for k in range(1, sizes[h]):
            ones[h, k].wait_recv()
            turn(h, k)
            pass_on(h, *along(h, k, 0))
    for k in range(max(sizes)):
        for h in range(2):
            if k < sizes[h]:
                for m in range(1, sizes[1 - h]):
                    twos[h, k, m].wait_recv()
                    pass_on(h, *along(h, k, m))
    for copy in twins.values():
        copy.wait_recv()
    for copy in list(ones.values()) + list(twos.values()) + list(twins.values()):
        copy.wait_send()


def states_before(overall, states):
    shards, mine = lax.axis_size("ctx"), lax.axis_index("ctx")
    wide = math.isqrt(shards // 2)
    tall = shards // 2 // wide
    most = max(wide, tall)
    heads, head_width, nstate = states.shape
    high = lax.reduce_precision(overall, 8, 7)
    tail = jnp.zeros((16, nstate), jnp.float32)
    tail = tail.at[0, :heads].set(high).at[1, :heads].set(overall - high)
    own = jnp.concatenate(
        [states.reshape(2, heads // 2 * head_width, nstate), jnp.stack([tail, tail])], axis=1
    ).astype(jnp.bfloat16)
    rows = own.shape[1]
    sems = pltpu.SemaphoreType.DMA
    vmem = pl.BlockSpec(memory_space=pltpu.VMEM)
    gathered = pl.pallas_call(
        functools.partial(state_kernel, wide, tall),
        out_shape=jax.ShapeDtypeStruct((2, shards, rows, nstate), jnp.bfloat16),
        in_specs=[vmem],
        out_specs=vmem,
        scratch_shapes=[
            sems((2, 2, most)),
            sems((2, 2, most, most)),
            sems((2, 2, wide, tall)),
        ],
        compiler_params=pltpu.CompilerParams(
            collective_id=1, has_side_effects=True, vmem_limit_bytes=40 * 1024 * 1024
        ),
    )(own)
    logs = gathered[0, :, rows - 16 : rows - 14, :heads].astype(jnp.float32)
    logs = logs[:, 0] + logs[:, 1]
    index = jnp.arange(shards)
    later = (index[None, :] > index[:, None]) & (index[None, :] < mine)
    fade = jnp.exp(jnp.sum(jnp.where(later[:, :, None], logs[None], 0.0), axis=1))
    fade = jnp.where((index < mine)[:, None], fade, 0.0)
    fade = fade.reshape(shards, 2, heads // 2).transpose(1, 0, 2)
    parts = gathered[:, :, : rows - 16].astype(jnp.float32)
    parts = parts.reshape(2, shards, heads // 2, head_width, nstate)
    before = jnp.sum(fade[:, :, :, None, None] * parts, axis=1)
    return before.reshape(heads, head_width, nstate)


def on_device(
    ssm_input,
    gate_input,
    key_proj,
    query_proj,
    step_size,
    decay_rate,
    head_gain,
    residual,
    ffn_gain,
    gate_weight,
    up_weight,
    down_weight,
    expert_ids,
    route_weight,
):
    head_count = step_size.shape[1]
    row_count, channels = ssm_input.shape
    head_width = channels // head_count
    within, running, overall, states = local_block(
        ssm_input, key_proj, query_proj, step_size, decay_rate, head_count
    )
    before = states_before(overall, states)
    carried = jnp.einsum(
        "th,hpn,tn->thp",
        jnp.exp(running),
        before,
        query_proj.astype(jnp.float32),
        precision=precise,
    )
    mixer_out = within + carried
    gated_out = mixer_out * jax.nn.silu(gate_input.astype(jnp.float32)).reshape(
        row_count, head_count, head_width
    )
    inv_rms = lax.rsqrt(jnp.mean(gated_out * gated_out, axis=2, keepdims=True) + 1e-05)
    normed = (gated_out * inv_rms).reshape(row_count, channels) * head_gain[None, :]
    block_out = (residual.astype(jnp.float32) + normed).astype(jnp.bfloat16)
    exp_count = lax.axis_size("exp")
    capacity = 3 * row_count // exp_count
    tables, gate_sum = route_tables(
        expert_ids, route_weight, jnp.arange(exp_count, dtype=jnp.int32), capacity
    )
    rows = exp_count * capacity
    picked = jnp.dot(
        tables.reshape(rows, row_count).astype(jnp.bfloat16),
        block_out,
        preferred_element_type=jnp.float32,
    ).astype(jnp.bfloat16)
    returned = expert_rows(
        picked.reshape(exp_count, capacity, channels),
        ffn_gain.reshape(exp_count, channels),
        gate_weight[0],
        up_weight[0],
        down_weight[0],
    )
    spread = jnp.einsum(
        "ekt,ekf->etf",
        tables.astype(jnp.bfloat16),
        returned,
        preferred_element_type=jnp.float32,
    )
    expert_out = jnp.sum(spread * gate_sum[:, :, None], axis=0).astype(jnp.bfloat16)
    return (block_out, expert_out)


def solution(mesh):
    placed = (
        P("ctx", "exp"),
        P("ctx", "exp"),
        P("ctx", None),
        P("ctx", None),
        P("ctx", "exp"),
        P("exp"),
        P("exp"),
        P("ctx", "exp"),
        P(),
        P("exp", None, "ctx"),
        P("exp", None, "ctx"),
        P("exp", "ctx", None),
        P("ctx", None),
        P("ctx", None),
    )
    return jax.shard_map(
        on_device,
        mesh=mesh,
        in_specs=placed,
        out_specs=(P("ctx", "exp"), P("ctx", "exp")),
        check_vma=False,
    )
```

```python
import functools
import math

import jax
import jax.numpy as jnp
from jax import lax
from jax.experimental import pallas as pl
from jax.experimental.pallas import tpu as pltpu
from jax.sharding import PartitionSpec as P

precise = lax.Precision.HIGHEST


def local_block(ssm_piece, key_piece, query_piece, step_piece, decay_rate, head_count):
    row_count = ssm_piece.shape[0]
    head_width = ssm_piece.shape[1] // head_count
    values = ssm_piece.astype(jnp.float32).reshape(row_count, head_count, head_width)
    key_vals = key_piece.astype(jnp.float32)
    queries = query_piece.astype(jnp.float32)
    log_steps = -step_piece * decay_rate[None, :]
    running = jnp.cumsum(log_steps, axis=0)
    scores = jnp.dot(queries, key_vals.T, precision=precise)
    causal = (jnp.arange(row_count)[:, None] >= jnp.arange(row_count)[None, :])[:, :, None]
    spacing = running[:, None, :] - running[None, :, :]
    decays = jnp.where(causal, jnp.exp(jnp.where(causal, spacing, 0.0)), 0.0)
    within = jnp.einsum("tsh,ts,shp->thp", decays, scores, values, precision=precise)
    overall = running[-1]
    fading = jnp.exp(overall[None, :] - running)
    states = jnp.einsum("sh,shp,sn->hpn", fading, values, key_vals, precision=precise)
    return (within, running, overall, states)


def route_tables(expert_ids, route_weight, experts, capacity):
    matched = expert_ids[None, :, :] == experts[:, None, None]
    member = jnp.any(matched, axis=2).astype(jnp.int32)
    gate_sum = jnp.sum(jnp.where(matched, route_weight[None, :, :], 0.0), axis=2)
    slot_index = jnp.cumsum(member, axis=1) - 1
    positions = jnp.arange(capacity, dtype=jnp.int32)
    routing = (
        (slot_index[:, None, :] == positions[None, :, None]) & (member[:, None, :] > 0)
    ).astype(jnp.float32)
    return (routing, gate_sum)


MESH = pl.DeviceIdType.MESH


def expert_kernel(
    wide,
    tall,
    picked_ref,
    gain_ref,
    gate_hbm,
    up_hbm,
    down_hbm,
    out_ref,
    arrived,
    rows_ref,
    gate_ref,
    up_ref,
    down_ref,
    hidden_ref,
    pair_ref,
    first_ref,
    second_ref,
    leaving,
    load_sem,
    in_sem,
    one_sem,
    two_sem,
    twin_sem,
    swap_sem,
    fold_sem,
    last_sem,
    out_sem,
):
    me, z = lax.axis_index("ctx"), lax.axis_index("exp")
    planes, count, width = picked_ref.shape
    half = rows_ref.shape[3]
    depth = gate_ref.shape[1]
    model = gate_ref.shape[0]
    core = lax.rem(me, 2)
    chip = me // 2
    x, y = lax.rem(chip, wide), chip // wide
    sizes = (wide, tall)
    pieces = 2 if count % 32 == 0 else 1
    piece = count // pieces

    def chip_at(i, j):
        return lax.rem(y + j + tall, tall) * wide + lax.rem(x + i + wide, wide)

    def ctx_at(i, j):
        return chip_at(i, j) * 2 + core

    def send(source, target, sem, index, where):
        return pltpu.make_async_remote_copy(
            src_ref=source,
            dst_ref=target,
            send_sem=sem.at[(0,) + index],
            recv_sem=sem.at[(1,) + index],
            device_id=where,
            device_id_type=MESH,
        )

    def along(h, first, second):
        return (first, second) if h == 0 else (second, first)

    loads = [
        pltpu.make_async_copy(gate_hbm, gate_ref, load_sem.at[0]),
        pltpu.make_async_copy(up_hbm, up_ref, load_sem.at[1]),
        pltpu.make_async_copy(down_hbm, down_ref, load_sem.at[2]),
    ]
    for load in loads:
        load.start()
    twin = {"ctx": me + 1 - 2 * core}
    partners = [twin]
    partners += [{"ctx": ctx_at(i, 0)} for i in range(1, wide)]
    partners += [{"ctx": ctx_at(0, j)} for j in range(1, tall)]
    partners += [{"exp": lax.rem(z + d, planes)} for d in range(1, planes)]
    barrier = pltpu.get_barrier_semaphore()
    for partner in partners:
        pl.semaphore_signal(barrier, inc=1, device_id=partner, device_id_type=MESH)
    pl.semaphore_wait(barrier, len(partners))

    def some(r):
        return pl.ds(r * piece, piece)

    inward = {}
    for r in range(pieces):
        for d in range(1, planes):
            goal = lax.rem(z + d, planes)
            inward[d, r] = send(
                picked_ref.at[goal, some(r)],
                arrived.at[z, some(r)],
                in_sem,
                (d, r),
                {"exp": goal},
            )
            inward[d, r].start()
    arrived[z] = picked_ref[z]
    ones, twos, twins = {}, {}, {}

    def pass_on(h, i, j, r):
        block = rows_ref.at[h, ctx_at(-i, -j), some(r)]
        twins[h, i, j, r] = send(block, block, twin_sem, (h, i, j, r), twin)
        twins[h, i, j, r].start()

    def turn(h, k, r):
        i, j = along(h, k, 0)
        block = rows_ref.at[h, ctx_at(-i, -j), some(r)]
        for m in range(1, sizes[1 - h]):
            a, b = along(h, 0, m)
            twos[h, k, m, r] = send(
                block, block, two_sem, (h, k, m, r), {"ctx": ctx_at(a, b)}
            )
            twos[h, k, m, r].start()

    for r in range(pieces):
        for d in range(1, planes):
            inward[d, r].wait_recv()
        total = jnp.zeros((piece, 1), jnp.float32)
        for s in range(planes):
            part = arrived[s, some(r)].astype(jnp.float32)
            total = total + jnp.sum(part * part, axis=1, keepdims=True)
        scale = lax.rsqrt(total / model + 1e-06)
        for s in range(planes):
            h, start = (s * width) // half, (s * width) % half
            rows_ref[h, me, some(r), start : start + width] = (
                arrived[s, some(r)].astype(jnp.float32) * scale * gain_ref[s : s + 1, :]
            ).astype(jnp.bfloat16)
        for h in range(2):
            for k in range(1, sizes[h]):
                i, j = along(h, k, 0)
                block = rows_ref.at[h, me, some(r)]
                ones[h, k, r] = send(
                    block, block, one_sem, (h, k, r), {"ctx": ctx_at(i, j)}
                )
                ones[h, k, r].start()
        for h in range(2):
            turn(h, 0, r)
        for h in range(2):
            pass_on(h, 0, 0, r)

    step = next(n for n in (512, 256, 128) if depth % n == 0)
    lane = 512 if half % 512 == 0 else 256

    def raise_rows(i, j):
        group = j * wide + i
        blocks = pl.ds(chip_at(-i, -j) * 2, 2)

        @pl.loop(0, depth // step)
        def _(t):
            cols = pl.ds(pl.multiple_of(t * step, step), step)

            def product(w_ref):
                value = None
                for h in range(2):
                    left = rows_ref[h, blocks].reshape(2 * count, half)
                    term = jnp.dot(
                        left,
                        w_ref[h * half : (h + 1) * half, cols],
                        preferred_element_type=jnp.float32,
                    )
                    value = term if value is None else value + term
                return value

            gate = product(gate_ref)
            hidden_ref[group, :, cols] = (gate * jax.nn.sigmoid(gate) * product(up_ref)).astype(
                jnp.bfloat16
            )

    order = sorted(
        [(i, j) for i in range(wide) for j in range(tall)], key=lambda o: (o[0] + o[1], o)
    )
    loads[0].wait()
    loads[1].wait()
    for r in range(pieces):
        for h in range(2):
            for k in range(1, sizes[h]):
                if r == 0:
                    ones[h, k, r].wait_recv()
                    turn(h, k, r)
                    pass_on(h, *along(h, k, 0), r)
    for r in range(pieces):
        for h in range(2):
            twins[h, 0, 0, r].wait_recv()
    raise_rows(0, 0)
    for r in range(1, pieces):
        for h in range(2):
            for k in range(1, sizes[h]):
                ones[h, k, r].wait_recv()
                turn(h, k, r)
                pass_on(h, *along(h, k, 0), r)
    for r in range(pieces):
        for h in range(2):
            for m in range(1, sizes[1 - h]):
                twos[h, 0, m, r].wait_recv()
                pass_on(h, *along(h, 0, m), r)
    for i, j in order[1:]:
        for r in range(pieces):
            for h in range(2):
                k, m = along(h, i, j)
                if k > 0 and m > 0:
                    twos[h, k, m, r].wait_recv()
                    pass_on(h, i, j, r)
        for r in range(pieces):
            for h in range(2):
                twins[h, i, j, r].wait_recv()
        raise_rows(i, j)
    for copy in list(ones.values()) + list(twos.values()) + list(twins.values()):
        copy.wait_send()

    swaps, folds, lasts = {}, {}, {}
    loads[2].wait()

    def lower_rows(i, j):
        group = ((tall - j) % tall) * wide + (wide - i) % wide
        base = chip_at(i, j) * 2
        for h in range(2):

            @pl.loop(0, half // lane)
            def _(t):
                cols = pl.ds(pl.multiple_of(t * lane, lane), lane)
                source = pl.ds(pl.multiple_of(h * half + t * lane, lane), lane)
                value = jnp.dot(
                    hidden_ref[group], down_ref[:, source], preferred_element_type=jnp.float32
                )
                rows_ref[h, pl.ds(base, 2), :, cols] = value.astype(jnp.bfloat16).reshape(
                    2, count, lane
                )

            swaps[h, i, j] = send(
                rows_ref.at[h, base + 1 - core],
                pair_ref.at[h, j * wide + i],
                swap_sem,
                (h, i, j),
                twin,
            )
            swaps[h, i, j].start()

    def add_into(target, other):
        @pl.loop(0, piece // 16)
        def _(t):
            few = pl.ds(pl.multiple_of(t * 16, 16), 16)
            target[few, :] = (
                target[few, :].astype(jnp.float32) + other[few, :].astype(jnp.float32)
            ).astype(jnp.bfloat16)

    def settle(i, j):
        for h in range(2):
            swaps[h, i, j].wait_recv()
        for r in range(pieces):
            for h in range(2):
                own = rows_ref.at[h, ctx_at(i, j), some(r)]
                add_into(own, pair_ref.at[h, j * wide + i, some(r)])
                k, m = along(h, i, j)
                if k > 0:
                    a, b = along(h, k, 0)
                    folds[h, k, m, r] = send(
                        own,
                        first_ref.at[h, k, m, some(r)],
                        fold_sem,
                        (h, k, m, r),
                        {"ctx": ctx_at(a, b)},
                    )
                    folds[h, k, m, r].start()

    goals = order[::-1]
    for number, goal in enumerate(goals):
        lower_rows(*goal)
        if number:
            settle(*goals[number - 1])
    settle(*goals[-1])
    for r in range(pieces):
        for h in range(2):
            major, minor = along(h, wide, tall)
            for m in range(1, minor):
                i, j = along(h, 0, m)
                own = rows_ref.at[h, ctx_at(i, j), some(r)]
                for k in range(1, major):
                    folds[h, k, m, r].wait_recv()
                    add_into(own, first_ref.at[h, k, m, some(r)])
                lasts[h, m, r] = send(
                    own,
                    second_ref.at[h, m, some(r)],
                    last_sem,
                    (h, m, r),
                    {"ctx": ctx_at(i, j)},
                )
                lasts[h, m, r].start()
    outward = {}
    for r in range(pieces):
        for h in range(2):
            own = rows_ref.at[h, me, some(r)]
            for k in range(1, sizes[h]):
                folds[h, k, 0, r].wait_recv()
                add_into(own, first_ref.at[h, k, 0, some(r)])
            for m in range(1, sizes[1 - h]):
                lasts[h, m, r].wait_recv()
                add_into(own, second_ref.at[h, m, some(r)])
        for s in range(planes):
            h, start = (s * width) // half, (s * width) % half
            leaving[s, some(r)] = rows_ref[h, me, some(r), start : start + width]
        for d in range(1, planes):
            goal = lax.rem(z + d, planes)
            outward[d, r] = send(
                leaving.at[goal, some(r)],
                out_ref.at[z, some(r)],
                out_sem,
                (d, r),
                {"exp": goal},
            )
            outward[d, r].start()
    out_ref[z] = leaving[z]
    for copy in outward.values():
        copy.wait_recv()
    for group in (inward, outward, swaps, folds, lasts):
        for copy in group.values():
            copy.wait_send()


def expert_rows(picked, gain, gate_here, up_here, down_here):
    shards, planes = lax.axis_size("ctx"), lax.axis_size("exp")
    chips = shards // 2
    wide = math.isqrt(chips)
    tall = chips // wide
    _, count, width = picked.shape
    model, depth = gate_here.shape
    half = model // 2
    most = max(wide, tall)
    vmem = pl.BlockSpec(memory_space=pltpu.VMEM)
    hbm = pl.BlockSpec(memory_space=pl.ANY)
    sems = pltpu.SemaphoreType.DMA
    return pl.pallas_call(
        functools.partial(expert_kernel, wide, tall),
        out_shape=jax.ShapeDtypeStruct((planes, count, width), jnp.bfloat16),
        in_specs=[vmem, vmem, hbm, hbm, hbm],
        out_specs=vmem,
        scratch_shapes=[
            pltpu.VMEM((planes, count, width), jnp.bfloat16),
            pltpu.VMEM((2, shards, count, half), jnp.bfloat16),
            pltpu.VMEM((model, depth), jnp.bfloat16),
            pltpu.VMEM((model, depth), jnp.bfloat16),
            pltpu.VMEM((depth, model), jnp.bfloat16),
            pltpu.VMEM((chips, 2 * count, depth), jnp.bfloat16),
            pltpu.VMEM((2, chips, count, half), jnp.bfloat16),
            pltpu.VMEM((2, most, most, count, half), jnp.bfloat16),
            pltpu.VMEM((2, most, count, half), jnp.bfloat16),
            pltpu.VMEM((planes, count, width), jnp.bfloat16),
            sems((3,)),
            sems((2, planes, 2)),
            sems((2, 2, most, 2)),
            sems((2, 2, most, most, 2)),
            sems((2, 2, wide, tall, 2)),
            sems((2, 2, wide, tall)),
            sems((2, 2, most, most, 2)),
            sems((2, 2, most, 2)),
            sems((2, planes, 2)),
        ],
        compiler_params=pltpu.CompilerParams(
            collective_id=0, has_side_effects=True, vmem_limit_bytes=60 * 1024 * 1024
        ),
        cost_estimate=pl.CostEstimate(
            flops=6 * shards * count * model * depth,
            bytes_accessed=6 * model * depth,
            transcendentals=shards * count * depth,
        ),
    )(picked, gain, gate_here, up_here, down_here)


def state_kernel(wide, tall, own_ref, all_ref, one_sem, two_sem, twin_sem):
    me = lax.axis_index("ctx")
    core = lax.rem(me, 2)
    chip = me // 2
    x, y = lax.rem(chip, wide), chip // wide
    sizes = (wide, tall)

    def ctx_at(i, j):
        return (lax.rem(y + j + tall, tall) * wide + lax.rem(x + i + wide, wide)) * 2 + core

    def send(block, sem, index, where):
        return pltpu.make_async_remote_copy(
            src_ref=block,
            dst_ref=block,
            send_sem=sem.at[(0,) + index],
            recv_sem=sem.at[(1,) + index],
            device_id=where,
            device_id_type=MESH,
        )

    def along(h, first, second):
        return (first, second) if h == 0 else (second, first)

    twin = {"ctx": me + 1 - 2 * core}
    partners = [twin]
    partners += [{"ctx": ctx_at(i, 0)} for i in range(1, wide)]
    partners += [{"ctx": ctx_at(0, j)} for j in range(1, tall)]
    barrier = pltpu.get_barrier_semaphore()
    for partner in partners:
        pl.semaphore_signal(barrier, inc=1, device_id=partner, device_id_type=MESH)
    for h in range(2):
        all_ref[h, me] = own_ref[h]
    pl.semaphore_wait(barrier, len(partners))
    ones, twos, twins = {}, {}, {}
    for h in range(2):
        for k in range(1, sizes[h]):
            i, j = along(h, k, 0)
            ones[h, k] = send(all_ref.at[h, me], one_sem, (h, k), {"ctx": ctx_at(i, j)})
            ones[h, k].start()

    def pass_on(h, i, j):
        twins[h, i, j] = send(all_ref.at[h, ctx_at(-i, -j)], twin_sem, (h, i, j), twin)
        twins[h, i, j].start()

    def turn(h, k):
        i, j = along(h, k, 0)
        block = all_ref.at[h, ctx_at(-i, -j)]
        for m in range(1, sizes[1 - h]):
            a, b = along(h, 0, m)
            twos[h, k, m] = send(block, two_sem, (h, k, m), {"ctx": ctx_at(a, b)})
            twos[h, k, m].start()

    for h in range(2):
        turn(h, 0)
    for h in range(2):
        pass_on(h, 0, 0)
    for h in range(2):
        for k in range(1, sizes[h]):
            ones[h, k].wait_recv()
            turn(h, k)
            pass_on(h, *along(h, k, 0))
    for k in range(max(sizes)):
        for h in range(2):
            if k < sizes[h]:
                for m in range(1, sizes[1 - h]):
                    twos[h, k, m].wait_recv()
                    pass_on(h, *along(h, k, m))
    for copy in twins.values():
        copy.wait_recv()
    for copy in list(ones.values()) + list(twos.values()) + list(twins.values()):
        copy.wait_send()


def states_before(overall, states):
    shards, mine = lax.axis_size("ctx"), lax.axis_index("ctx")
    wide = math.isqrt(shards // 2)
    tall = shards // 2 // wide
    most = max(wide, tall)
    heads, head_width, nstate = states.shape
    high = lax.reduce_precision(overall, 8, 7)
    tail = jnp.zeros((16, nstate), jnp.float32)
    tail = tail.at[0, :heads].set(high).at[1, :heads].set(overall - high)
    own = jnp.concatenate(
        [states.reshape(2, heads // 2 * head_width, nstate), jnp.stack([tail, tail])], axis=1
    ).astype(jnp.bfloat16)
    rows = own.shape[1]
    sems = pltpu.SemaphoreType.DMA
    vmem = pl.BlockSpec(memory_space=pltpu.VMEM)
    gathered = pl.pallas_call(
        functools.partial(state_kernel, wide, tall),
        out_shape=jax.ShapeDtypeStruct((2, shards, rows, nstate), jnp.bfloat16),
        in_specs=[vmem],
        out_specs=vmem,
        scratch_shapes=[
            sems((2, 2, most)),
            sems((2, 2, most, most)),
            sems((2, 2, wide, tall)),
        ],
        compiler_params=pltpu.CompilerParams(
            collective_id=1, has_side_effects=True, vmem_limit_bytes=40 * 1024 * 1024
        ),
    )(own)
    logs = gathered[0, :, rows - 16 : rows - 14, :heads].astype(jnp.float32)
    logs = logs[:, 0] + logs[:, 1]
    index = jnp.arange(shards)
    later = (index[None, :] > index[:, None]) & (index[None, :] < mine)
    fade = jnp.exp(jnp.sum(jnp.where(later[:, :, None], logs[None], 0.0), axis=1))
    fade = jnp.where((index < mine)[:, None], fade, 0.0)
    fade = fade.reshape(shards, 2, heads // 2).transpose(1, 0, 2)
    parts = gathered[:, :, : rows - 16].astype(jnp.float32)
    parts = parts.reshape(2, shards, heads // 2, head_width, nstate)
    before = jnp.sum(fade[:, :, :, None, None] * parts, axis=1)
    return before.reshape(heads, head_width, nstate)


def on_device(
    ssm_input,
    gate_input,
    key_proj,
    query_proj,
    step_size,
    decay_rate,
    head_gain,
    residual,
    ffn_gain,
    gate_weight,
    up_weight,
    down_weight,
    expert_ids,
    route_weight,
):
    head_count = step_size.shape[1]
    row_count, channels = ssm_input.shape
    head_width = channels // head_count
    within, running, overall, states = local_block(
        ssm_input, key_proj, query_proj, step_size, decay_rate, head_count
    )
    before = states_before(overall, states)
    carried = jnp.einsum(
        "th,hpn,tn->thp",
        jnp.exp(running),
        before,
        query_proj.astype(jnp.float32),
        precision=precise,
    )
    mixer_out = within + carried
    gated_out = mixer_out * jax.nn.silu(gate_input.astype(jnp.float32)).reshape(
        row_count, head_count, head_width
    )
    inv_rms = lax.rsqrt(jnp.mean(gated_out * gated_out, axis=2, keepdims=True) + 1e-05)
    normed = (gated_out * inv_rms).reshape(row_count, channels) * head_gain[None, :]
    block_out = (residual.astype(jnp.float32) + normed).astype(jnp.bfloat16)
    exp_count = lax.axis_size("exp")
    capacity = 3 * row_count // exp_count
    tables, gate_sum = route_tables(
        expert_ids, route_weight, jnp.arange(exp_count, dtype=jnp.int32), capacity
    )
    rows = exp_count * capacity
    picked = jnp.dot(
        tables.reshape(rows, row_count).astype(jnp.bfloat16),
        block_out,
        preferred_element_type=jnp.float32,
    ).astype(jnp.bfloat16)
    returned = expert_rows(
        picked.reshape(exp_count, capacity, channels),
        ffn_gain.reshape(exp_count, channels),
        gate_weight[0],
        up_weight[0],
        down_weight[0],
    )
    spread = jnp.einsum(
        "ekt,ekf->etf",
        tables.astype(jnp.bfloat16),
        returned,
        preferred_element_type=jnp.float32,
    )
    expert_out = jnp.sum(spread * gate_sum[:, :, None], axis=0).astype(jnp.bfloat16)
    return (block_out, expert_out)


def solution(mesh):
    placed = (
        P("ctx", "exp"),
        P("ctx", "exp"),
        P("ctx", None),
        P("ctx", None),
        P("ctx", "exp"),
        P("exp"),
        P("exp"),
        P("ctx", "exp"),
        P(),
        P("exp", None, "ctx"),
        P("exp", None, "ctx"),
        P("exp", "ctx", None),
        P("ctx", None),
        P("ctx", None),
    )
    return jax.shard_map(
        on_device,
        mesh=mesh,
        in_specs=placed,
        out_specs=(P("ctx", "exp"), P("ctx", "exp")),
        check_vma=False,
    )
```
